256 devices in a mesh: expert: 64 (over z, y, core), mp: 4 (over x).
Axes of the slice: x: 4, y: 4, z: 8, core: 2. Of those that a mesh axis runs over, the one named last changes fastest.
Arguments:
- tokens: bfloat16 [16384, 2048], P('expert'), may hold values from -6 to 6
- out_grad: bfloat16 [16384, 2048], P('expert'), may hold values from -6 to 6
- expert_ids: int32 [16384, 1], P('expert'), may hold values from 0 to 31; in each aligned block of 256 rows (0 to 255, 256 to 511, ...) at most 16 rows name the same one
- w_in: bfloat16 [64, 2048, 2560], P('expert', None, 'mp'), may hold values from -0.125 to 0.125
- w_out: bfloat16 [64, 2560, 2048], P('expert', 'mp'), may hold values from -0.078125 to 0.078125
- in_row_mom: float32 [64, 1024], P('expert'), may hold values from 0.2 to 5
- in_col_mom: float32 [64, 2560], P('expert', 'mp'), may hold values from 0.2 to 5
- out_row_mom: float32 [64, 2560], P('expert', 'mp'), may hold values from 0.2 to 5
- out_col_mom: float32 [64, 1024], P('expert'), may hold values from 0.2 to 5
Outputs:
- token_grad: bfloat16 [16384, 2048], P('expert', 'mp')
- w_in_new: bfloat16 [64, 2048, 2560], P('expert', None, 'mp')
- w_out_new: bfloat16 [64, 2560, 2048], P('expert', 'mp')
- in_row_new: float32 [64, 1024], P('expert')
- in_col_new: float32 [64, 2560], P('expert', 'mp')
- out_row_new: float32 [64, 2560], P('expert', 'mp')
- out_col_new: float32 [64, 1024], P('expert')
The draws below stay inside these ranges and needn't reach their ends.
Inputs may be any that keep to these rules, and one draw needn't show every extreme that they name: `expert_ids`: in the 256 tokens of one index of the expert axis (aligned blocks of rows) no expert is named more than 16 times, a bound that some block reaches.
All inputs are finite; a program needn't handle non-finite values.
Results may differ from the reference program's by a relative error of at most 0.0045.
The reference program's roundings to bfloat16 on the way (of `active` and `pre_grad`) count: a program that leaves them out, or rounds other values in their place, can miss the bound.
Values may be sent and summed in bfloat16 or wider, within the bound.
A program may use at most 128 MiB of HBM per device.

```python
import math
import jax
import jax.numpy as jnp
import numpy as np
from jax import lax

D = 2048
FF = 5120
TOK_DEV = 256
EXPERTS = 32
CAP = 16
TOKENS = 16384
N_EXPERT = 64


def block_scale(stream_key, extent, shards, smallest, largest):
    def one(position, shards_of):
        draws = jax.random.uniform(jax.random.fold_in(jax.random.fold_in(stream_key, 6), position), (shards_of,), jnp.float32, smallest / len(shards), largest / len(shards))
        return jnp.repeat(jnp.exp(draws), extent[position] // shards_of).reshape((-1,) + (1,) * (len(extent) - position - 1))

    factor_of = one(*shards[0])
    for cut in shards[1:]:
        factor_of = factor_of * one(*cut)
    return factor_of


def shared_out(key, own, number, rows, count, top, bound, lean):
    ranking = jax.random.permutation(key, count)
    crowded, ordinary = shares(count, rows * top, bound, lean, True), shares(count, rows * top, bound, lean, False)
    places = jnp.arange(count)

    def named(tallies, rotation):
        used = int((tallies > 0).sum())
        fixed = max(1, used // 4)
        shifted = fixed + (places - fixed + rotation * (used - fixed)) % max(1, count - fixed)
        return jnp.zeros((count,), jnp.int32).at[ranking[jnp.where(places < fixed, places, shifted)]].set(jnp.asarray(tallies, jnp.int32))

    tallies = jnp.where(number % 4 == 0, named(crowded, number // 4), named(ordinary, number - number // 4 - 1))
    mixed = jax.random.permutation(jax.random.fold_in(own, 3), count)
    giver, sink = mixed[0:count // 2 * 2:2], mixed[1:count // 2 * 2:2]
    room = jnp.minimum(tallies[giver] - 1, bound - tallies[sink]) // 2
    room = jnp.where((giver == ranking[0]) | (sink == ranking[0]) | (tallies[sink] == 0), 0, jnp.maximum(room, 0))
    shifted = jax.random.randint(jax.random.fold_in(own, 4), (count // 2,), 0, 1 << 20) % (room + 1)
    tallies = tallies.at[giver].add(-shifted).at[sink].add(shifted)
    members = jnp.searchsorted(jnp.cumsum(tallies), jnp.arange(rows * top), side="right").astype(jnp.int32)
    listing = members.reshape(top, rows).T
    listing = listing[jax.random.permutation(jax.random.fold_in(own, 1), rows)]
    rotation = jax.random.randint(jax.random.fold_in(own, 2), (rows, 1), 0, top)
    return jnp.take_along_axis(listing, (jnp.arange(top)[None, :] + rotation) % top, axis=1)


def shares(amount, total, bound, lean, full):
    portions = [(1 << 20) // math.isqrt(standing ** lean) + 1 for standing in range(1, amount + 1)]
    largest = bound if full else min(bound, max(-(-total // amount), total * portions[0] // sum(portions)))
    least = 1 if total - largest >= amount - 1 else 0
    counts, rest = [largest] + [least] * (amount - 1), total - largest - least * (amount - 1)
    while rest > 0:
        movable = [i for i in range(1, amount) if counts[i] < largest] or [i for i in range(1, amount) if counts[i] < bound]
        mass, remaining = sum([portions[i] for i in movable]), rest
        for i in movable:
            addition = min(bound - counts[i], max(1, remaining * portions[i] // mass), rest)
            counts[i] = counts[i] + addition
            rest = rest - addition
    return np.array(counts)


def gaussian(key, dims, deviation, most, pieces=(), held_as=jnp.bfloat16):
    factor_of = block_scale(key, dims, pieces, -0.22, 0.18) if pieces else 1.0
    result = jax.random.normal(key, dims, jnp.float32) * deviation * factor_of
    return jnp.minimum(jnp.maximum(result, -most), most).astype(held_as)


def setup_inputs(seed: int = 0) -> dict:
    streams_of = jax.random.split(jax.random.key(seed), 10)
    tokens = gaussian(streams_of[0], (TOKENS, D), 1.0, 6.0, ((0, 64),))
    out_grad = gaussian(streams_of[1], (TOKENS, D), 1.0, 6.0, ((0, 64),))
    expert_ids_keys = jax.random.split(jax.random.fold_in(streams_of[2], 1), TOKENS // TOK_DEV)
    expert_ids_turns = jax.random.permutation(jax.random.fold_in(streams_of[2], 3), TOKENS // TOK_DEV)
    expert_ids = jax.vmap(lambda own, number: shared_out(jax.random.fold_in(streams_of[2], 2), own, number, TOK_DEV, EXPERTS, 1, CAP, 2))(expert_ids_keys, expert_ids_turns).reshape((TOKENS, 1))
    w_in = gaussian(streams_of[3], (2 * EXPERTS, D, FF // 2), D ** -0.5, 0.125, ((0, 64), (2, 4)))
    w_out = gaussian(streams_of[4], (2 * EXPERTS, FF // 2, D), FF ** -0.5, 0.078125, ((0, 64), (1, 4)))
    in_row_mom = jnp.clip(jnp.exp(math.log(5.0) - 3.218876 * jax.random.uniform(streams_of[5], (2 * EXPERTS, D // 2), jnp.float32) ** block_scale(streams_of[5], (2 * EXPERTS, D // 2), ((0, 64),), -0.2, 0.2)), 0.2, 5.0)
    in_col_mom = jnp.clip(jnp.exp(math.log(5.0) - 3.218876 * jax.random.uniform(streams_of[6], (2 * EXPERTS, FF // 2), jnp.float32) ** block_scale(streams_of[6], (2 * EXPERTS, FF // 2), ((0, 64), (1, 4)), -0.2, 0.2)), 0.2, 5.0)
    out_row_mom = jnp.clip(jnp.exp(math.log(5.0) - 3.218876 * jax.random.uniform(streams_of[7], (2 * EXPERTS, FF // 2), jnp.float32) ** block_scale(streams_of[7], (2 * EXPERTS, FF // 2), ((0, 64), (1, 4)), -0.2, 0.2)), 0.2, 5.0)
    out_col_mom = jnp.clip(jnp.exp(math.log(5.0) - 3.218876 * jax.random.uniform(streams_of[8], (2 * EXPERTS, D // 2), jnp.float32) ** block_scale(streams_of[8], (2 * EXPERTS, D // 2), ((0, 64),), -0.2, 0.2)), 0.2, 5.0)
    return dict(tokens=tokens, out_grad=out_grad, expert_ids=expert_ids, w_in=w_in, w_out=w_out, in_row_mom=in_row_mom, in_col_mom=in_col_mom, out_row_mom=out_row_mom, out_col_mom=out_col_mom)


beta_two = 0.8
step_size = 0.01
epsilon_one = 1e-30

def gelu_pair(preact, upstream):
    active, pull = jax.vjp(jax.nn.gelu, preact)
    return (active, pull(upstream)[0])

def matmul(left, right):
    return jnp.dot(left.astype(jnp.float32), right.astype(jnp.float32), precision=lax.Precision.HIGHEST, preferred_element_type=jnp.float32)

def factored(gradient, weight, old_row, old_column, clip_factor):
    scaled = clip_factor * gradient
    square = scaled * scaled + epsilon_one
    row_new = beta_two * old_row + (1.0 - beta_two) * lax.optimization_barrier(jnp.mean(square, axis=1))
    column_new = beta_two * old_column + (1.0 - beta_two) * lax.optimization_barrier(jnp.mean(square, axis=0))
    second = row_new[:, None] * column_new[None, :] / jnp.mean(row_new)
    updated = (weight.astype(jnp.float32) - step_size * clip_factor * gradient / jnp.sqrt(second)).astype(jnp.bfloat16)
    return (updated, row_new, column_new)

def reference(tokens, out_grad, expert_ids, w_in, w_out, in_row_mom, in_col_mom, out_row_mom, out_col_mom):
    rows_per = N_EXPERT * CAP
    chosen = expert_ids[:, 0].astype(jnp.int32)
    onehot = (chosen[:, None] == jnp.arange(EXPERTS, dtype=jnp.int32)[None, :]).astype(jnp.int32)
    blocks = onehot.reshape(N_EXPERT, TOK_DEV, EXPERTS)
    earlier = (jnp.cumsum(blocks, axis=1) - blocks).reshape(TOKENS, EXPERTS)
    rank_in = lax.optimization_barrier(jnp.sum(earlier * onehot, axis=1)).astype(jnp.int32)
    anchor = jnp.arange(TOKENS, dtype=jnp.int32) // TOK_DEV
    slot_index = (anchor * CAP + rank_in).astype(jnp.int32)
    source = jnp.full((EXPERTS, rows_per), TOKENS, jnp.int32).at[chosen, slot_index].set(jnp.arange(TOKENS, dtype=jnp.int32))
    w_full = w_in.reshape(EXPERTS, 2, D, FF // 2).transpose(0, 2, 1, 3).reshape(EXPERTS, D, FF)
    v_full = w_out.reshape(EXPERTS, FF, D)

    def local_pass(expert_index):
        picked = source[expert_index]
        tok_rows = jnp.take(tokens, picked, axis=0, mode='fill', fill_value=0)
        grad_rows = jnp.take(out_grad, picked, axis=0, mode='fill', fill_value=0)
        w_expert = w_full[expert_index]
        v_expert = v_full[expert_index]
        preact = matmul(tok_rows, w_expert)
        upstream = matmul(grad_rows, v_expert.T)
        active, pre_grad = gelu_pair(preact, upstream)
        active = active.astype(jnp.bfloat16)
        pre_grad = pre_grad.astype(jnp.bfloat16)
        gradient_in = matmul(tok_rows.T, pre_grad)
        gradient_out = matmul(active.T, grad_rows)
        return (pre_grad, gradient_in, gradient_out, w_expert, v_expert)

    def first_pass(expert_index):
        pre_grad, gradient_in, gradient_out, w_expert, v_expert = local_pass(expert_index)
        rows_grad = matmul(pre_grad, w_expert.T).astype(jnp.bfloat16)
        squares = jnp.sum(gradient_in * gradient_in) + jnp.sum(gradient_out * gradient_out)
        return (rows_grad, squares)
    stacked, squares = lax.map(first_pass, jnp.arange(EXPERTS, dtype=jnp.int32))
    token_grad = stacked[chosen, slot_index]
    norm_total = jnp.sum(squares)
    param_total = 2.0 * EXPERTS * D * FF
    clip_factor = jnp.minimum(1.0, jnp.sqrt(param_total / norm_total))

    def second_pass(operands):
        expert_index, old_in_row, old_in_column, old_out_row, old_out_column = operands
        pre_grad, gradient_in, gradient_out, w_expert, v_expert = local_pass(expert_index)
        new_w, in_row, in_column = factored(gradient_in, w_expert, old_in_row, old_in_column, clip_factor)
        new_v, out_row, out_column = factored(gradient_out, v_expert, old_out_row, old_out_column, clip_factor)
        return (new_w, new_v, in_row, in_column, out_row, out_column)
    new_w, new_v, in_row, in_column, out_row, out_column = lax.map(second_pass, (jnp.arange(EXPERTS, dtype=jnp.int32), in_row_mom.reshape(EXPERTS, D), in_col_mom.reshape(EXPERTS, FF), out_row_mom.reshape(EXPERTS, FF), out_col_mom.reshape(EXPERTS, D)))
    w_in_new = new_w.reshape(EXPERTS, D, 2, FF // 2).transpose(0, 2, 1, 3).reshape(2 * EXPERTS, D, FF // 2)
    w_out_new = new_v.reshape(2 * EXPERTS, FF // 2, D)
    return (token_grad, w_in_new, w_out_new, in_row.reshape(2 * EXPERTS, D // 2), in_column.reshape(2 * EXPERTS, FF // 2), out_row.reshape(2 * EXPERTS, FF // 2), out_column.reshape(2 * EXPERTS, D // 2))
```

```python
import functools

import jax
import jax.numpy as jnp
from jax import lax
from jax.experimental import pallas as pl
from jax.experimental.pallas import tpu as pltpu
from jax.sharding import PartitionSpec as P

MESH = pl.DeviceIdType.MESH
F32 = jnp.float32
BF16 = jnp.bfloat16
CHIPS_Y = 4
CAP = 16
beta_two = 0.8
step_size = 0.01
epsilon_one = 1e-30
root_two_over_pi = 0.7978845608028654


def dot(left, right, contract):
    return lax.dot_general(left, right, (contract, ((), ())), preferred_element_type=F32)


def kernel(
    sizes,
    tok_hbm, grad_hbm, ids_ref, w_hbm, v_hbm, irm_ref, icm_ref, orm_ref, ocm_ref,
    tg_ref, wn_hbm, vn_hbm, irn_ref, icn_ref, orn_ref, ocn_ref,
    tokq, gradq, place, packed, buf, w_v, v_v, g_in, g_out, pre_s, up_s, act_s, pg_s,
    tkeep, tsend, trecv, sown, d2s, d2r, nbs, nbr, fin, rbuf, pbuf, nbuf, rs_in, rs_out, a_in, a_out,
    load_sem, a2a_ss, a2a_rs, x1_ss, x1_rs, x2_ss, x2_rs, cf_ss, cf_rs, tc_ss, tc_rs,
    d2_ss, d2_rs, nb_ss, nb_rs, ret_ss, ret_rs, st1_ss, st1_rs, st2_ss, st2_rs, out_sem,
):
    T, D, H, Z, Y = sizes
    K = Z * Y
    NCH = Z // 2
    DQ, DH = D // 4, D // 2
    RG = Y * CAP
    RK = 2 * RG
    R = 2 * RK
    FF = 8 * H
    e = lax.axis_index("expert")
    x = lax.axis_index("mp")
    k = e // 2
    c = e % 2
    z = k // Y
    y = k % Y
    xr, xo, xl = (x + 1) % 4, (x + 2) % 4, (x + 3) % 4
    quarter = (x, xr, xo, xl)
    right, left, core = (e, xr), (e, xl), (2 * k + 1 - c, x)

    def remote(src, dst, ss, rs, dev):
        return pltpu.make_async_remote_copy(
            src_ref=src, dst_ref=dst, send_sem=ss, recv_sem=rs, device_id=dev, device_id_type=MESH
        )

    def expert_at(dz, dy):
        return ((z + dz + Z) % Z) * Y + (y + dy + Y) % Y

    def dz_of(ch, jj):
        return -ch if jj == 0 else ch + 1

    def rows(cr, jj):
        return pl.ds(cr * RK + jj * RG, RG)

    def slots(expert):
        return pl.ds(pl.multiple_of(expert * CAP, CAP), CAP)

    def a2a(ch, jj, dy):
        to = expert_at(dz_of(ch, jj), dy)
        return remote(
            packed.at[:, slots(to), :],
            buf.at[x, ch, :, pl.ds(jj * RG + dy * CAP, CAP), :],
            a2a_ss.at[2 * ch + jj, dy], a2a_rs.at[2 * ch + jj, dy], (2 * to + c, x),
        )

    def x1(ch, jj, way, q):
        here = buf.at[q, ch, :, rows(0, jj), :]
        return remote(
            here, here, x1_ss.at[2 * ch + jj, way], x1_rs.at[2 * ch + jj, way], (right, left)[way]
        )

    def x2(ch, jj, way, q):
        here = buf.at[q, ch, way, rows(0, jj), :]
        return remote(
            here, here, x2_ss.at[2 * ch + jj, way], x2_rs.at[2 * ch + jj, way], (right, left)[way]
        )

    def cf(ch, jj, rq):
        return remote(
            buf.at[quarter[rq], ch, :, rows(0, jj), :],
            buf.at[quarter[rq], ch, :, rows(1, jj), :],
            cf_ss.at[2 * ch + jj, rq], cf_rs.at[2 * ch + jj, rq], core,
        )

    def tc(ch):
        return remote(tsend.at[ch], trecv.at[ch], tc_ss.at[ch], tc_rs.at[ch], core)

    def d2(ch, way):
        return remote(
            d2s.at[ch, way], d2r.at[ch, way], d2_ss.at[ch, way], d2_rs.at[ch, way], (right, left)[way]
        )

    def nb(ch, way):
        return remote(
            nbs.at[ch, way], nbr.at[ch, way], nb_ss.at[ch, way], nb_rs.at[ch, way], (right, left)[way]
        )

    def ret(ch, jj, dy, landing):
        to = expert_at(-dz_of(ch, jj), -dy)
        return remote(
            fin.at[ch, pl.ds(jj * RG + dy * CAP, CAP), :],
            rbuf.at[slots(landing), :],
            ret_ss.at[2 * ch + jj, dy], ret_rs.at[2 * ch + jj, dy], (2 * to + c, x),
        )

    def st1(dx, dc, slot):
        to = (2 * k + (c + dc) % 2, (x + dx) % 4)
        return remote(
            pbuf.at[slot], pbuf.at[slot], st1_ss.at[dx, dc], st1_rs.at[dx, dc], to
        )

    def st2(off, slot):
        to = (2 * ((k + off) % K) + c, x)
        return remote(nbuf.at[slot], nbuf.at[slot], st2_ss.at[off], st2_rs.at[off], to)

    columns = pl.ds(pl.multiple_of(x * DQ, DQ), DQ)
    loads = [
        pltpu.make_async_copy(tok_hbm.at[:, columns], tokq, load_sem.at[0]),
        pltpu.make_async_copy(grad_hbm.at[:, columns], gradq, load_sem.at[1]),
        pltpu.make_async_copy(w_hbm.at[0], w_v, load_sem.at[2]),
        pltpu.make_async_copy(v_hbm.at[0], v_v, load_sem.at[3]),
    ]
    for load in loads:
        load.start()
    barrier = pltpu.get_barrier_semaphore()
    column_peers = [(dx, dc) for dx in range(4) for dc in range(2) if dx or dc]
    for off in range(1, K):
        pl.semaphore_signal(
            barrier, inc=1, device_id=(2 * ((k + off) % K) + c, x), device_id_type=MESH
        )
    for dx, dc in column_peers:
        pl.semaphore_signal(
            barrier, inc=1, device_id=(2 * k + (c + dc) % 2, (x + dx) % 4), device_id_type=MESH
        )

    lanes = max(128, K)
    chosen = ids_ref[...]
    onehot = jnp.where(lax.broadcasted_iota(jnp.int32, (T, lanes), 1) == chosen, 1.0, 0.0)
    below = jnp.where(
        lax.broadcasted_iota(jnp.int32, (T, T), 0) > lax.broadcasted_iota(jnp.int32, (T, T), 1), 1.0, 0.0
    )
    earlier = dot(below.astype(BF16), onehot.astype(BF16), ((1,), (0,)))
    rank = jnp.sum(earlier * onehot, axis=1, keepdims=True)
    slot = chosen * CAP + rank.astype(jnp.int32)
    place[...] = jnp.where(
        lax.broadcasted_iota(jnp.int32, (T, K * CAP), 1) == slot, 1.0, 0.0
    ).astype(BF16)
    loads[0].wait()
    packed[0] = dot(place[...], tokq[...], ((0,), (0,))).astype(BF16)
    loads[1].wait()
    packed[1] = dot(place[...], gradq[...], ((0,), (0,))).astype(BF16)
    pl.semaphore_wait(barrier, K - 1 + len(column_peers))

    every = [(ch, jj, dy) for ch in range(NCH) for jj in range(2) for dy in range(Y)][1:]
    for ch, jj, dy in every:
        a2a(ch, jj, dy).start()
    own = pltpu.make_async_copy(
        packed.at[:, slots(k), :], buf.at[x, 0, :, pl.ds(0, CAP), :], load_sem.at[4]
    )
    own.start()
    g_in[...] = jnp.zeros_like(g_in)
    g_out[...] = jnp.zeros_like(g_out)

    def step_a(ch, jj, first=False):
        for dy in range(Y):
            if first and dy == 0:
                own.wait()
            else:
                a2a(ch, jj, dy).wait_recv()
        x1(ch, jj, 0, x).start()
        x1(ch, jj, 1, x).start()
        cf(ch, jj, 0).start()

    def step_b(ch, jj):
        x1(ch, jj, 0, xl).wait_recv()
        x2(ch, jj, 0, xl).start()
        x1(ch, jj, 1, xr).wait_recv()
        x2(ch, jj, 1, xr).start()
        cf(ch, jj, 3).start()
        cf(ch, jj, 1).start()

    def step_c(ch, jj):
        x2(ch, jj, 0, xo).wait_recv()
        x2(ch, jj, 1, xo).wait_recv()
        cf(ch, jj, 2).start()

    def step_d(ch):
        for jj in range(2):
            for rq in range(4):
                cf(ch, jj, rq).wait_recv()

    def forward(ch):
        for q in range(4):
            part = slice(q * DQ, (q + 1) * DQ)
            pre = dot(buf[q, ch, 0], w_v[part, :], ((1,), (0,)))
            up = dot(buf[q, ch, 1], v_v[:, part], ((1,), (1,)))
            pre_s[...] = pre if q == 0 else pre_s[...] + pre
            up_s[...] = up if q == 0 else up_s[...] + up

        def activate(i, carry):
            some = pl.ds(pl.multiple_of(i * 32, 32), 32)
            p = pre_s[some, :]
            square = p * p
            tanh = jnp.tanh(root_two_over_pi * (p + 0.044715 * (p * square)))
            cdf = 0.5 * (1.0 + tanh)
            slope = cdf + (0.5 * root_two_over_pi) * p * (1.0 - tanh * tanh) * (
                1.0 + (3.0 * 0.044715) * square
            )
            act_s[some, :] = (p * cdf).astype(BF16)
            pg_s[some, :] = (up_s[some, :] * slope).astype(BF16)
            return carry

        lax.fori_loop(0, R // 32, activate, 0)
        for q in range(4):
            part = slice(q * DQ, (q + 1) * DQ)
            t = dot(pg_s[...], w_v[part, :], ((1,), (1,)))
            tsend[ch, q] = t[RK:].astype(BF16)
            tkeep[q] = t[:RK]
        tc(ch).start()

    def grads_in(ch):
        for q in range(4):
            part = slice(q * DQ, (q + 1) * DQ)
            g_in[part, :] += dot(buf[q, ch, 0], pg_s[...], ((0,), (0,)))

    def grads_out(ch):
        for q in range(4):
            part = slice(q * DQ, (q + 1) * DQ)
            g_out[:, part] += dot(act_s[...], buf[q, ch, 1], ((0,), (0,)))

    def step_r2(ch):
        tc(ch).wait_recv()
        both = tkeep[xo] + trecv[ch, xo].astype(F32)
        d2s[ch, 0] = both[:RG].astype(BF16)
        d2s[ch, 1] = both[RG:].astype(BF16)
        d2(ch, 0).start()
        d2(ch, 1).start()
        sown[ch] = tkeep[x] + trecv[ch, x].astype(F32)

    def step_r3(ch):
        d2(ch, 0).wait_recv()
        to_right = tkeep[xr] + trecv[ch, xr].astype(F32)
        nbs[ch, 0, :RG] = (to_right[:RG] + d2r[ch, 0].astype(F32)).astype(BF16)
        nbs[ch, 0, RG:] = to_right[RG:].astype(BF16)
        nb(ch, 0).start()
        d2(ch, 1).wait_recv()
        to_left = tkeep[xl] + trecv[ch, xl].astype(F32)
        nbs[ch, 1, :RG] = to_left[:RG].astype(BF16)
        nbs[ch, 1, RG:] = (to_left[RG:] + d2r[ch, 1].astype(F32)).astype(BF16)
        nb(ch, 1).start()

    def step_r4(ch):
        nb(ch, 0).wait_recv()
        nb(ch, 1).wait_recv()
        fin[ch] = (sown[ch] + nbr[ch, 0].astype(F32) + nbr[ch, 1].astype(F32)).astype(BF16)
        for jj in range(2):
            for dy in range(Y):
                if jj or dy:
                    ret(ch, jj, dy, k).start()

        @pl.when(ch > 0)
        def _():
            ret(ch, 0, 0, k).start()

        @pl.when(ch == 0)
        def _():
            rbuf[slots(k), :] = fin[0, :CAP, :]

    def also(condition, *steps):
        @pl.when(condition)
        def _():
            for function, *args in steps:
                function(*args)

    step_a(0, 0, first=True)
    step_a(0, 1)
    step_b(0, 0)
    step_a(1, 0)
    step_b(0, 1)
    step_c(0, 0)
    step_a(1, 1)
    step_b(1, 0)
    step_c(0, 1)
    loads[2].wait()
    loads[3].wait()

    def chunk(ch, carry):
        also(ch + 2 < NCH, (step_a, ch + 2, 0))
        also(ch + 1 < NCH, (step_b, ch + 1, 1), (step_c, ch + 1, 0))
        step_d(ch)
        forward(ch)
        also(ch > 0, (step_r4, ch - 1))
        also(ch + 2 < NCH, (step_a, ch + 2, 1), (step_b, ch + 2, 0))
        grads_in(ch)
        step_r2(ch)
        also(ch + 1 < NCH, (step_c, ch + 1, 1))
        grads_out(ch)
        step_r3(ch)
        return carry

    lax.fori_loop(0, NCH, chunk, 0)

    def squares_in(i, total):
        some = pl.ds(pl.multiple_of(i * 128, 128), 128)
        g = g_in[some, :]
        s = g * g
        narrow = s[:, :128]
        for t in range(1, H // 128):
            narrow = narrow + s[:, t * 128 : (t + 1) * 128]
        rs_in[:, some] = jnp.sum(narrow.T, axis=0, keepdims=True)
        return total + jnp.sum(s.reshape(16, 8, H), axis=0)

    def squares_out(i, total):
        some = pl.ds(pl.multiple_of(i * 128, 128), 128)
        g = g_out[some, :]
        s = g * g
        narrow = s[:, :128]
        for t in range(1, D // 128):
            narrow = narrow + s[:, t * 128 : (t + 1) * 128]
        rs_out[:, some] = jnp.sum(narrow.T, axis=0, keepdims=True)
        return total + jnp.sum(s.reshape(16, 8, D), axis=0)

    cs_in = jnp.sum(
        lax.fori_loop(0, D // 128, squares_in, jnp.zeros((8, H), F32)), axis=0, keepdims=True
    )
    cs_out = jnp.sum(
        lax.fori_loop(0, H // 128, squares_out, jnp.zeros((8, D), F32)), axis=0, keepdims=True
    )

    def total_of(row):
        return jnp.sum(row, axis=1, keepdims=True)

    mine = x * 2 + c
    norm_part = total_of(cs_in) + total_of(cs_out)
    pbuf[mine, 0:1] = rs_in[:, :DH]
    pbuf[mine, 1:2] = rs_in[:, DH:]
    pbuf[mine, 2:3] = cs_out[:, :DH]
    pbuf[mine, 3:4] = cs_out[:, DH:]
    pbuf[mine, 4:5] = irm_ref[...]
    pbuf[mine, 5:6] = ocm_ref[...]
    pbuf[mine, 6:7] = jnp.broadcast_to(norm_part, (1, DH))
    pbuf[mine, 7:8, : DH // 2] = jnp.broadcast_to(total_of(orm_ref[...]), (1, DH // 2))
    pbuf[mine, 7:8, DH // 2 :] = jnp.broadcast_to(total_of(rs_out[...]), (1, DH // 2))
    for dx, dc in column_peers:
        st1(dx, dc, mine).start()
    step_r4(NCH - 1)
    for dx, dc in column_peers:
        st1(dx, dc, ((x - dx + 4) % 4) * 2 + (c + dc) % 2).wait_recv()
    sums = pbuf[0]
    for s in range(1, 8):
        sums = sums + pbuf[s]
    nbuf[k] = jnp.broadcast_to(sums[6:7, :128], (8, 128))
    for off in range(1, K):
        st2(off, k).start()

    for ch, jj, dy in every:
        ret(ch, jj, dy, expert_at(dz_of(ch, jj), dy)).wait_recv()
    tg_ref[...] = dot(place[...], rbuf[...], ((1,), (0,))).astype(BF16)

    for off in range(1, K):
        st2(off, (k - off + K) % K).wait_recv()
    norm_total = jnp.sum(nbuf[...], axis=0)[0:1, 0:1]
    clip = jnp.minimum(1.0, jnp.sqrt((2.0 * K * D * FF) / norm_total))
    clip_two = clip * clip
    zero, one = pbuf[x * 2], pbuf[x * 2 + 1]
    old_in_row = jnp.concatenate([zero[4:5], one[4:5]], axis=1)
    old_out_col = jnp.concatenate([zero[5:6], one[5:6]], axis=1)
    row_in = jnp.concatenate([sums[0:1], sums[1:2]], axis=1)
    col_out = jnp.concatenate([sums[2:3], sums[3:4]], axis=1)

    def moved(old, squares, count):
        return beta_two * old + (1.0 - beta_two) * (clip_two * (squares / count) + epsilon_one)

    in_row = moved(old_in_row, row_in, FF)
    in_col = moved(icm_ref[...], cs_in, D)
    out_row = moved(orm_ref[...], rs_out[...], D)
    out_col = moved(old_out_col, col_out, FF)
    mean_in = total_of(in_row) / D
    mean_out = moved(sums[7:8, 0:1] / FF, sums[7:8, DH // 2 : DH // 2 + 1] / D, FF)
    irn_ref[...] = jnp.where(c == 0, in_row[:, :DH], in_row[:, DH:])
    ocn_ref[...] = jnp.where(c == 0, out_col[:, :DH], out_col[:, DH:])
    icn_ref[...] = in_col
    orn_ref[...] = out_row
    a_in[...] = (step_size * clip * jnp.sqrt(mean_in)) * lax.rsqrt(in_row)
    a_out[...] = (step_size * clip * jnp.sqrt(mean_out)) * lax.rsqrt(out_row)
    b_in = lax.rsqrt(in_col)
    b_out = lax.rsqrt(out_col)

    def update(weight, gradient, a, b, width):
        def block(i, carry):
            some = pl.ds(pl.multiple_of(i * 128, 128), 128)
            scale = jnp.broadcast_to(a[:, some], (128, 128)).T
            for t in range(width // 128):
                part = slice(t * 128, (t + 1) * 128)
                moved_by = gradient[some, part] * scale * b[:, part]
                weight[some, part] = (weight[some, part].astype(F32) - moved_by).astype(BF16)
            return carry

        return block

    outs = []
    update_in = update(w_v, g_in, a_in, b_in, H)
    for q in range(4):
        lax.fori_loop(q * DQ // 128, (q + 1) * DQ // 128, update_in, 0)
        part = pl.ds(q * DQ, DQ)
        outs.append(pltpu.make_async_copy(w_v.at[part, :], wn_hbm.at[0, part, :], out_sem.at[q]))
        outs[-1].start()
    update_out = update(v_v, g_out, a_out, b_out, D)
    for i in range(H // 128):
        update_out(i, 0)
        part = pl.ds(i * 128, 128)
        outs.append(pltpu.make_async_copy(v_v.at[part, :], vn_hbm.at[0, part, :], out_sem.at[4 + i]))
        outs[-1].start()

    for ch, jj, dy in every:
        a2a(ch, jj, dy).wait_send()
        ret(ch, jj, dy, k).wait_send()
    for ch in range(NCH):
        tc(ch).wait_send()
        for way in range(2):
            d2(ch, way).wait_send()
            nb(ch, way).wait_send()
            for jj in range(2):
                x1(ch, jj, way, x).wait_send()
                x2(ch, jj, way, (xl, xr)[way]).wait_send()
        for jj in range(2):
            for rq in range(4):
                cf(ch, jj, rq).wait_send()
    for dx, dc in column_peers:
        st1(dx, dc, mine).wait_send()
    for off in range(1, K):
        st2(off, k).wait_send()
    for out in outs:
        out.wait()


def shards(
    tokens, out_grad, expert_ids, w_in, w_out, in_row_mom, in_col_mom, out_row_mom, out_col_mom
):
    T, D = tokens.shape
    H = w_in.shape[2]
    K = lax.axis_size("expert") // 2
    Y = CHIPS_Y
    Z = K // Y
    NCH, DQ = Z // 2, D // 4
    RG = Y * CAP
    RK, R = 2 * RG, 4 * RG
    hbm = pl.BlockSpec(memory_space=pl.ANY)
    vmem = pl.BlockSpec(memory_space=pltpu.VMEM)
    dma = pltpu.SemaphoreType.DMA
    scratch = [
        pltpu.VMEM((T, DQ), BF16),
        pltpu.VMEM((T, DQ), BF16),
        pltpu.VMEM((T, K * CAP), BF16),
        pltpu.VMEM((2, K * CAP, DQ), BF16),
        pltpu.VMEM((4, NCH, 2, R, DQ), BF16),
        pltpu.VMEM((D, H), BF16),
        pltpu.VMEM((H, D), BF16),
        pltpu.VMEM((D, H), F32),
        pltpu.VMEM((H, D), F32),
        pltpu.VMEM((R, H), F32),
        pltpu.VMEM((R, H), F32),
        pltpu.VMEM((R, H), BF16),
        pltpu.VMEM((R, H), BF16),
        pltpu.VMEM((4, RK, DQ), F32),
        pltpu.VMEM((NCH, 4, RK, DQ), BF16),
        pltpu.VMEM((NCH, 4, RK, DQ), BF16),
        pltpu.VMEM((NCH, RK, DQ), F32),
        pltpu.VMEM((NCH, 2, RG, DQ), BF16),
        pltpu.VMEM((NCH, 2, RG, DQ), BF16),
        pltpu.VMEM((NCH, 2, RK, DQ), BF16),
        pltpu.VMEM((NCH, 2, RK, DQ), BF16),
        pltpu.VMEM((NCH, RK, DQ), BF16),
        pltpu.VMEM((K * CAP, DQ), BF16),
        pltpu.VMEM((8, 8, D // 2), F32),
        pltpu.VMEM((K, 8, 128), F32),
        pltpu.VMEM((1, D), F32),
        pltpu.VMEM((1, H), F32),
        pltpu.VMEM((1, D), F32),
        pltpu.VMEM((1, H), F32),
        dma((5,)),
        dma((Z, Y)), dma((Z, Y)),
        dma((Z, 2)), dma((Z, 2)),
        dma((Z, 2)), dma((Z, 2)),
        dma((Z, 4)), dma((Z, 4)),
        dma((NCH,)), dma((NCH,)),
        dma((NCH, 2)), dma((NCH, 2)),
        dma((NCH, 2)), dma((NCH, 2)),
        dma((Z, Y)), dma((Z, Y)),
        dma((4, 2)), dma((4, 2)),
        dma((K,)), dma((K,)),
        dma((4 + H // 128,)),
    ]
    return pl.pallas_call(
        functools.partial(kernel, (T, D, H, Z, Y)),
        out_shape=(
            jax.ShapeDtypeStruct((T, DQ), BF16),
            jax.ShapeDtypeStruct(w_in.shape, BF16),
            jax.ShapeDtypeStruct(w_out.shape, BF16),
            jax.ShapeDtypeStruct(in_row_mom.shape, F32),
            jax.ShapeDtypeStruct(in_col_mom.shape, F32),
            jax.ShapeDtypeStruct(out_row_mom.shape, F32),
            jax.ShapeDtypeStruct(out_col_mom.shape, F32),
        ),
        in_specs=[hbm, hbm, vmem, hbm, hbm, vmem, vmem, vmem, vmem],
        out_specs=(vmem, hbm, hbm, vmem, vmem, vmem, vmem),
        scratch_shapes=scratch,
        compiler_params=pltpu.CompilerParams(
            collective_id=0, has_side_effects=True, vmem_limit_bytes=56 * 1024 * 1024
        ),
    )(tokens, out_grad, expert_ids, w_in, w_out, in_row_mom, in_col_mom, out_row_mom, out_col_mom)


def solution(mesh):
    placed = (
        P("expert", None),
        P("expert", None),
        P("expert", None),
        P("expert", None, "mp"),
        P("expert", "mp", None),
        P("expert", None),
        P("expert", "mp"),
        P("expert", "mp"),
        P("expert", None),
    )
    return jax.shard_map(
        shards,
        mesh=mesh,
        in_specs=placed,
        out_specs=(
            P("expert", "mp"),
            P("expert", None, "mp"),
            P("expert", "mp", None),
            P("expert", None),
            P("expert", "mp"),
            P("expert", "mp"),
            P("expert", None),
        ),
        check_vma=False,
    )
```

```python
import functools

import jax
import jax.numpy as jnp
from jax import lax
from jax.experimental import pallas as pl
from jax.experimental.pallas import tpu as pltpu
from jax.sharding import PartitionSpec as P

MESH = pl.DeviceIdType.MESH
F32 = jnp.float32
BF16 = jnp.bfloat16
CHIPS_Y = 4
CAP = 16
beta_two = 0.8
step_size = 0.01
epsilon_one = 1e-30
root_two_over_pi = 0.7978845608028654


def dot(left, right, contract):
    return lax.dot_general(left, right, (contract, ((), ())), preferred_element_type=F32)


def plan_of(chunks):
    if chunks == 2:
        body = [(["D0"], ["C1"], ["20"]), (["D1"], ["30 40"], ["21"])]
        return ["S1 A0 B0", "A1 C0 B1"], body, (["31"], ["41"])
    body = [
        (["D0"], ["C1 A3 B2"], ["20"]),
        (["D1"], ["B3 C2 30"], ["C3 21"]),
        (["D2"], ["40 31"], ["22"]),
        (["D3"], ["41 32"], ["23"]),
    ]
    return ["S1 A0 B0", "S2 A1 C0", "B1 A2 S3"], body, (["33 42"], ["43"])


def kernel(
    sizes,
    tok_hbm, grad_hbm, ids_ref, w_hbm, v_hbm, irm_ref, icm_ref, orm_ref, ocm_ref,
    tg_ref, wn_hbm, vn_hbm, irn_ref, icn_ref, orn_ref, ocn_ref,
    tok_v, place, packed, packed_row, buf, w_v, v_v, g_in, g_out, pre_s, up_s, act_s, pg_s,
    tkeep, tsend, trecv, sown, d2s, d2r, nbs, nbr, fin, rbuf, mom_s, mom_r, pbuf, nbuf, rs_out, a_in, a_out,
    load_sem, own_sem, mom_ss, mom_rs, a2a_ss, a2a_rs, row_ss, row_rs, cfr_ss, cfr_rs, x1_ss, x1_rs, x2_ss, x2_rs, cf_ss, cf_rs, tc_ss, tc_rs,
    d2_ss, d2_rs, nb_ss, nb_rs, ret_ss, ret_rs, st1_ss, st1_rs, st2_ss, st2_rs, out_sem,
):
    T, D, H, Z, Y = sizes
    K = Z * Y
    NCH = Z // 2
    DQ, DH = D // 4, D // 2
    RG = Y * CAP
    RK = 2 * RG
    R = 2 * RK
    FF = 8 * H
    e = lax.axis_index("expert")
    x = lax.axis_index("mp")
    k = e // 2
    c = e % 2
    z = k // Y
    y = k % Y
    xr, xo, xl = (x + 1) % 4, (x + 2) % 4, (x + 3) % 4
    quarter = (x, xr, xo, xl)
    right, left, core = (e, xr), (e, xl), (2 * k + 1 - c, x)

    def remote(src, dst, ss, rs, dev):
        return pltpu.make_async_remote_copy(
            src_ref=src, dst_ref=dst, send_sem=ss, recv_sem=rs, device_id=dev, device_id_type=MESH
        )

    def expert_at(dz, dy):
        return ((z + dz + Z) % Z) * Y + (y + dy + Y) % Y

    last = NCH - 1

    def dz_of(ch, jj):
        return ch + 1 if jj == 0 else -(ch + 1) * (1 - (ch + 1) // NCH)

    def rows(cr, jj):
        return pl.ds(cr * RK + jj * RG, RG)

    def slots(expert):
        return pl.ds(pl.multiple_of(expert * CAP, CAP), CAP)

    def a2a(ch, jj, dy):
        to = expert_at(dz_of(ch, jj), dy)
        return remote(
            packed.at[:, slots(to), :],
            buf.at[x, ch, :, pl.ds(jj * RG + dy * CAP, CAP), :],
            a2a_ss.at[2 * ch + jj, dy], a2a_rs.at[2 * ch + jj, dy], (2 * to + c, x),
        )

    def own_row(dy):
        to = (y + dy) % Y
        return remote(
            packed_row.at[:, :, slots(to), :],
            buf.at[:, last, :, pl.ds(RG + dy * CAP, CAP), :],
            row_ss.at[dy], row_rs.at[dy], (2 * (z * Y + to) + c, x),
        )

    def cf_row():
        return remote(
            buf.at[:, last, :, rows(0, 1), :], buf.at[:, last, :, rows(1, 1), :],
            cfr_ss.at[0], cfr_rs.at[0], core,
        )

    def mom():
        return remote(mom_s, mom_r, mom_ss.at[0], mom_rs.at[0], core)

    def x1(ch, jj, way, q):
        here = buf.at[q, ch, :, rows(0, jj), :]
        return remote(
            here, here, x1_ss.at[2 * ch + jj, way], x1_rs.at[2 * ch + jj, way], (right, left)[way]
        )

    def x2(ch, jj, way, q):
        here = buf.at[q, ch, way, rows(0, jj), :]
        return remote(
            here, here, x2_ss.at[2 * ch + jj, way], x2_rs.at[2 * ch + jj, way], (right, left)[way]
        )

    def cf(ch, jj, rq):
        return remote(
            buf.at[quarter[rq], ch, :, rows(0, jj), :],
            buf.at[quarter[rq], ch, :, rows(1, jj), :],
            cf_ss.at[2 * ch + jj, rq], cf_rs.at[2 * ch + jj, rq], core,
        )

    def tc(ch):
        return remote(tsend.at[ch], trecv.at[ch], tc_ss.at[ch], tc_rs.at[ch], core)

    def d2(ch, way):
        return remote(
            d2s.at[ch, way], d2r.at[ch, way], d2_ss.at[ch, way], d2_rs.at[ch, way], (right, left)[way]
        )

    def nb(ch, way):
        return remote(
            nbs.at[ch, way], nbr.at[ch, way], nb_ss.at[ch, way], nb_rs.at[ch, way], (right, left)[way]
        )

    def ret(ch, jj, dy, landing):
        to = expert_at(-dz_of(ch, jj), -dy)
        return remote(
            fin.at[ch, pl.ds(jj * RG + dy * CAP, CAP), :],
            rbuf.at[slots(landing), :],
            ret_ss.at[2 * ch + jj, dy], ret_rs.at[2 * ch + jj, dy], (2 * to + c, x),
        )

    def st1(dx, dc, slot):
        to = (2 * k + (c + dc) % 2, (x + dx) % 4)
        return remote(
            pbuf.at[slot], pbuf.at[slot], st1_ss.at[dx, dc], st1_rs.at[dx, dc], to
        )

    def st2(off, slot):
        to = (2 * ((k + off) % K) + c, x)
        return remote(nbuf.at[slot], nbuf.at[slot], st2_ss.at[off], st2_rs.at[off], to)

    loads = []
    for a, whole in enumerate((tok_hbm, grad_hbm)):
        for q in range(4):
            loads.append(
                pltpu.make_async_copy(
                    whole.at[:, pl.ds(q * DQ, DQ)], tok_v.at[a, q], load_sem.at[4 * a + q]
                )
            )
    loads.append(pltpu.make_async_copy(w_hbm.at[0], w_v, load_sem.at[8]))
    loads.append(pltpu.make_async_copy(v_hbm.at[0], v_v, load_sem.at[9]))
    for load in loads:
        load.start()
    barrier = pltpu.get_barrier_semaphore()
    column_peers = [(dx, dc) for dx in range(4) for dc in range(2) if dx or dc]
    for off in range(1, K):
        pl.semaphore_signal(
            barrier, inc=1, device_id=(2 * ((k + off) % K) + c, x), device_id_type=MESH
        )
    for dx, dc in column_peers:
        pl.semaphore_signal(
            barrier, inc=1, device_id=(2 * k + (c + dc) % 2, (x + dx) % 4), device_id_type=MESH
        )

    lanes = max(128, K)
    chosen = jnp.broadcast_to(ids_ref[...].astype(F32), (128, T)).T[:, :1]
    onehot = jnp.where(
        lax.broadcasted_iota(jnp.int32, (T, lanes), 1).astype(F32) == chosen, 1.0, 0.0
    )
    below = jnp.where(
        lax.broadcasted_iota(jnp.int32, (T, T), 0) > lax.broadcasted_iota(jnp.int32, (T, T), 1), 1.0, 0.0
    )
    earlier = dot(below.astype(BF16), onehot.astype(BF16), ((1,), (0,)))
    rank = jnp.sum(earlier * onehot, axis=1, keepdims=True)
    slot = (chosen * CAP + rank).astype(jnp.int32)
    place[...] = jnp.where(
        lax.broadcasted_iota(jnp.int32, (T, K * CAP), 1) == slot, 1.0, 0.0
    ).astype(BF16)
    for load in loads[:8]:
        load.wait()
    for a in range(2):
        packed[a] = dot(place[...], tok_v[a, x], ((0,), (0,))).astype(BF16)
    mom_s[:, :DH] = irm_ref[...]
    mom_s[:, DH:] = ocm_ref[...]
    pl.semaphore_wait(barrier, K - 1 + len(column_peers))

    halves = [(ch, jj) for ch in range(NCH) for jj in range(2)][:-1]
    away = [(ch, jj, dy) for ch, jj in halves for dy in range(Y)]
    row_peers = range(1, Y)

    def send(ch, jj):
        for dy in range(Y):
            a2a(ch, jj, dy).start()

    def sent(ch, jj):
        for dy in range(Y):
            a2a(ch, jj, dy).wait_send()

    send(0, 0)
    send(0, 1)
    mom().start()
    row_lanes = max(128, RG)
    row_place = jnp.where(
        lax.broadcasted_iota(jnp.int32, (T, row_lanes), 1) + z * RG == slot, 1.0, 0.0
    ).astype(BF16)
    for q in range(4):
        for a in range(2):
            packed_row[q, a] = dot(row_place, tok_v[a, q], ((0,), (0,)))[:RG].astype(BF16)
    for dy in row_peers:
        own_row(dy).start()
    own = pltpu.make_async_copy(
        packed_row.at[:, :, slots(y), :], buf.at[:, last, :, pl.ds(RG, CAP), :], own_sem.at[0]
    )
    own.start()
    g_in[...] = jnp.zeros_like(g_in)
    g_out[...] = jnp.zeros_like(g_out)

    def step_a(ch, jj):
        for dy in range(Y):
            a2a(ch, jj, dy).wait_recv()
        x1(ch, jj, 0, x).start()
        x1(ch, jj, 1, x).start()
        cf(ch, jj, 0).start()

    def step_a_row():
        own.wait()
        for dy in row_peers:
            own_row(dy).wait_recv()
        cf_row().start()

    def step_b(ch, jj):
        x1(ch, jj, 0, xl).wait_recv()
        x2(ch, jj, 0, xl).start()
        x1(ch, jj, 1, xr).wait_recv()
        x2(ch, jj, 1, xr).start()
        cf(ch, jj, 3).start()
        cf(ch, jj, 1).start()

    def step_c(ch, jj):
        x2(ch, jj, 0, xo).wait_recv()
        x2(ch, jj, 1, xo).wait_recv()
        cf(ch, jj, 2).start()

    def step_d(ch, jj):
        for rq in range(4):
            cf(ch, jj, rq).wait_recv()

    def step_d_row():
        cf_row().wait_recv()

    def forward(ch):
        for q in range(4):
            part = slice(q * DQ, (q + 1) * DQ)
            pre = dot(buf[q, ch, 0], w_v[part, :], ((1,), (0,)))
            up = dot(buf[q, ch, 1], v_v[:, part], ((1,), (1,)))
            pre_s[...] = pre if q == 0 else pre_s[...] + pre
            up_s[...] = up if q == 0 else up_s[...] + up

        def activate(i, carry):
            some = pl.ds(pl.multiple_of(i * 32, 32), 32)
            p = pre_s[some, :]
            square = p * p
            tanh = jnp.tanh(root_two_over_pi * (p + 0.044715 * (p * square)))
            cdf = 0.5 * (1.0 + tanh)
            slope = cdf + (0.5 * root_two_over_pi) * p * (1.0 - tanh * tanh) * (
                1.0 + (3.0 * 0.044715) * square
            )
            act_s[some, :] = (p * cdf).astype(BF16)
            pg_s[some, :] = (up_s[some, :] * slope).astype(BF16)
            return carry

        lax.fori_loop(0, R // 32, activate, 0)
        for q in range(4):
            part = slice(q * DQ, (q + 1) * DQ)
            t = dot(pg_s[...], w_v[part, :], ((1,), (1,)))
            tsend[ch, q] = t[RK:].astype(BF16)
            tkeep[ch, q] = t[:RK]
        tc(ch).start()

    def grads_in(ch):
        for q in range(4):
            part = slice(q * DQ, (q + 1) * DQ)
            g_in[part, :] += dot(buf[q, ch, 0], pg_s[...], ((0,), (0,)))

    def grads_out(ch):
        for q in range(4):
            part = slice(q * DQ, (q + 1) * DQ)
            g_out[:, part] += dot(act_s[...], buf[q, ch, 1], ((0,), (0,)))

    def step_r2(ch):
        tc(ch).wait_recv()
        both = tkeep[ch, xo] + trecv[ch, xo].astype(F32)
        d2s[ch, 0] = both[:RG].astype(BF16)
        d2s[ch, 1] = both[RG:].astype(BF16)
        d2(ch, 0).start()
        d2(ch, 1).start()
        sown[ch] = tkeep[ch, x] + trecv[ch, x].astype(F32)

    def step_r3(ch):
        d2(ch, 0).wait_recv()
        to_right = tkeep[ch, xr] + trecv[ch, xr].astype(F32)
        nbs[ch, 0, :RG] = (to_right[:RG] + d2r[ch, 0].astype(F32)).astype(BF16)
        nbs[ch, 0, RG:] = to_right[RG:].astype(BF16)
        nb(ch, 0).start()
        d2(ch, 1).wait_recv()
        to_left = tkeep[ch, xl] + trecv[ch, xl].astype(F32)
        nbs[ch, 1, :RG] = to_left[:RG].astype(BF16)
        nbs[ch, 1, RG:] = (to_left[RG:] + d2r[ch, 1].astype(F32)).astype(BF16)
        nb(ch, 1).start()

    def step_r4(ch):
        nb(ch, 0).wait_recv()
        nb(ch, 1).wait_recv()
        fin[ch] = (sown[ch] + nbr[ch, 0].astype(F32) + nbr[ch, 1].astype(F32)).astype(BF16)
        for jj in range(2):
            for dy in range(Y):
                if dy or not jj:
                    ret(ch, jj, dy, k).start()

        if ch < last:
            ret(ch, 1, 0, k).start()
        else:
            rbuf[slots(k), :] = fin[last, RG : RG + CAP, :]

    def stage(n, step, row_step=None):
        if 0 <= n < NCH:
            step(n, 0)
        if 0 <= n < last:
            step(n, 1)
        if n == last and row_step is not None:
            row_step()

    def send_after(n):
        stage(n - 1, sent)
        stage(n, send)

    def later(n, step):
        if 0 <= n < NCH:
            step(n)

    def act(name, n):
        if name == "S":
            send_after(n)
        elif name == "A":
            stage(n, step_a, step_a_row)
        elif name == "B":
            stage(n, step_b)
        elif name == "C":
            stage(n, step_c)
        elif name == "D":
            stage(n, step_d, step_d_row)
        else:
            later(n, {"2": step_r2, "3": step_r3, "4": step_r4}[name])

    def run(plan):
        for word in " ".join(plan).split():
            act(word[0], int(word[1:]))

    before, body, after = plan_of(NCH)
    run(before)
    loads[8].wait()
    loads[9].wait()

    def during(ch, part):
        for n, parts in enumerate(body):
            if parts[part]:
                pl.when(ch == n)(functools.partial(run, parts[part]))

    def chunk(ch, carry):
        during(ch, 0)
        forward(ch)
        during(ch, 1)
        grads_in(ch)
        grads_out(ch)
        during(ch, 2)
        return carry

    lax.fori_loop(0, NCH, chunk, 0)

    mine = x * 2 + c

    def squares_in(i, total):
        some = pl.ds(pl.multiple_of(i * 128, 128), 128)
        g = g_in[some, :]
        s = g * g
        narrow = s[:, :128]
        for t in range(1, H // 128):
            narrow = narrow + s[:, t * 128 : (t + 1) * 128]
        pbuf[mine, :, some] = jnp.sum(narrow.T, axis=0, keepdims=True)
        return total + jnp.sum(s.reshape(16, 8, H), axis=0)

    def squares_out(i, total):
        some = pl.ds(pl.multiple_of(i * 128, 128), 128)
        g = g_out[some, :]
        s = g * g
        narrow = s[:, :128]
        for t in range(1, D // 128):
            narrow = narrow + s[:, t * 128 : (t + 1) * 128]
        rs_out[:, some] = jnp.sum(narrow.T, axis=0, keepdims=True)
        return total + jnp.sum(s.reshape(16, 8, D), axis=0)

    cs_in = jnp.sum(
        lax.fori_loop(0, D // 128, squares_in, jnp.zeros((8, H), F32)), axis=0, keepdims=True
    )
    cs_out = jnp.sum(
        lax.fori_loop(0, H // 128, squares_out, jnp.zeros((8, D), F32)), axis=0, keepdims=True
    )

    def total_of(row):
        return jnp.sum(row, axis=1, keepdims=True)

    pbuf[mine, :, D : 2 * D] = cs_out
    scalars = (total_of(cs_in) + total_of(cs_out), total_of(orm_ref[...]), total_of(rs_out[...]))
    for i, scalar in enumerate(scalars):
        pbuf[mine, :, 2 * D + i * 128 : 2 * D + (i + 1) * 128] = jnp.broadcast_to(scalar, (1, 128))
    for dx, dc in column_peers:
        st1(dx, dc, mine).start()
    run(after[0])
    for dx, dc in column_peers:
        st1(dx, dc, ((x - dx + 4) % 4) * 2 + (c + dc) % 2).wait_recv()
    sums = pbuf[0]
    for s in range(1, 8):
        sums = sums + pbuf[s]
    nbuf[k] = sums[:, 2 * D : 2 * D + 128]
    for off in range(1, K):
        st2(off, k).start()
    run(after[1])

    for off in range(1, K):
        st2(off, (k - off + K) % K).wait_recv()
    norm_total = jnp.sum(nbuf[...], axis=0)[0:1, 0:1]
    clip = jnp.minimum(1.0, jnp.sqrt((2.0 * K * D * FF) / norm_total))
    clip_two = clip * clip
    mom().wait_recv()
    mom_own, mom_other = mom_s[...], mom_r[...]
    mom_zero = jnp.where(c == 0, mom_own, mom_other)
    mom_one = jnp.where(c == 0, mom_other, mom_own)
    old_in_row = jnp.concatenate([mom_zero[:, :DH], mom_one[:, :DH]], axis=1)
    old_out_col = jnp.concatenate([mom_zero[:, DH:], mom_one[:, DH:]], axis=1)
    row_in, col_out = sums[:, :D], sums[:, D : 2 * D]

    def moved(old, squares, count):
        return beta_two * old + (1.0 - beta_two) * (clip_two * (squares / count) + epsilon_one)

    in_row = moved(old_in_row, row_in, FF)
    in_col = moved(icm_ref[...], cs_in, D)
    out_row = moved(orm_ref[...], rs_out[...], D)
    out_col = moved(old_out_col, col_out, FF)
    mean_in = total_of(in_row) / D
    mean_out = moved(sums[:, 2 * D + 128 : 2 * D + 129] / FF, sums[:, 2 * D + 256 : 2 * D + 257] / D, FF)
    irn_ref[...] = jnp.where(c == 0, in_row[:, :DH], in_row[:, DH:])
    ocn_ref[...] = jnp.where(c == 0, out_col[:, :DH], out_col[:, DH:])
    icn_ref[...] = in_col
    orn_ref[...] = out_row
    a_in[...] = (step_size * clip * jnp.sqrt(mean_in)) * lax.rsqrt(in_row)
    a_out[...] = (step_size * clip * jnp.sqrt(mean_out)) * lax.rsqrt(out_row)
    b_in = lax.rsqrt(in_col)
    b_out = lax.rsqrt(out_col)

    def update(weight, gradient, a, b, width):
        def block(i, carry):
            some = pl.ds(pl.multiple_of(i * 128, 128), 128)
            scale = jnp.broadcast_to(a[:, some], (128, 128)).T
            for t in range(width // 128):
                part = slice(t * 128, (t + 1) * 128)
                moved_by = gradient[some, part] * scale * b[:, part]
                weight[some, part] = (weight[some, part].astype(F32) - moved_by).astype(BF16)
            return carry

        return block

    outs = []
    update_in = update(w_v, g_in, a_in, b_in, H)
    for q in range(4):
        lax.fori_loop(q * DQ // 128, (q + 1) * DQ // 128, update_in, 0)
        part = pl.ds(q * DQ, DQ)
        outs.append(pltpu.make_async_copy(w_v.at[part, :], wn_hbm.at[0, part, :], out_sem.at[q]))
        outs[-1].start()
    update_out = update(v_v, g_out, a_out, b_out, D)
    for i in range(H // 128):
        update_out(i, 0)
        part = pl.ds(i * 128, 128)
        outs.append(pltpu.make_async_copy(v_v.at[part, :], vn_hbm.at[0, part, :], out_sem.at[4 + i]))
        outs[-1].start()

    back = away + [(last, 1, dy) for dy in row_peers]
    for ch, jj, dy in back:
        ret(ch, jj, dy, expert_at(dz_of(ch, jj), dy)).wait_recv()
    tg_ref[...] = dot(place[...], rbuf[...], ((1,), (0,))).astype(BF16)

    stage(last, sent)
    mom().wait_send()
    cf_row().wait_send()
    for ch, jj, dy in back:
        ret(ch, jj, dy, k).wait_send()
    for dy in row_peers:
        own_row(dy).wait_send()
    for ch in range(NCH):
        tc(ch).wait_send()
        for way in range(2):
            d2(ch, way).wait_send()
            nb(ch, way).wait_send()
    for ch, jj in halves:
        for way in range(2):
            x1(ch, jj, way, x).wait_send()
            x2(ch, jj, way, (xl, xr)[way]).wait_send()
        for rq in range(4):
            cf(ch, jj, rq).wait_send()
    for dx, dc in column_peers:
        st1(dx, dc, mine).wait_send()
    for off in range(1, K):
        st2(off, k).wait_send()
    for out in outs:
        out.wait()


def deliver(*refs):
    sem = refs[14]
    copies = []
    for i, (src, dst) in enumerate(zip(refs[:7], refs[7:14])):
        cuts = 4 if i in (1, 2) else 1
        size = src.shape[1] // cuts
        for part in range(cuts):
            at = (slice(None), pl.ds(part * size, size)) if cuts > 1 else (slice(None),) * 2
            copies.append(pltpu.make_async_copy(src.at[at], dst.at[at], sem.at[len(copies)]))
            copies[-1].start()
    for copy in copies:
        copy.wait()


def shards(
    tokens, out_grad, expert_ids, w_in, w_out, in_row_mom, in_col_mom, out_row_mom, out_col_mom
):
    T, D = tokens.shape
    H = w_in.shape[2]
    K = lax.axis_size("expert") // 2
    Y = CHIPS_Y
    Z = K // Y
    NCH, DQ = Z // 2, D // 4
    RG = Y * CAP
    RK, R = 2 * RG, 4 * RG
    hbm = pl.BlockSpec(memory_space=pl.ANY)
    vmem = pl.BlockSpec(memory_space=pltpu.VMEM)
    dma = pltpu.SemaphoreType.DMA
    scratch = [
        pltpu.VMEM((2, 4, T, DQ), BF16),
        pltpu.VMEM((T, K * CAP), BF16),
        pltpu.VMEM((2, K * CAP, DQ), BF16),
        pltpu.VMEM((4, 2, RG, DQ), BF16),
        pltpu.VMEM((4, NCH, 2, R, DQ), BF16),
        pltpu.VMEM((D, H), BF16),
        pltpu.VMEM((H, D), BF16),
        pltpu.VMEM((D, H), F32),
        pltpu.VMEM((H, D), F32),
        pltpu.VMEM((R, H), F32),
        pltpu.VMEM((R, H), F32),
        pltpu.VMEM((R, H), BF16),
        pltpu.VMEM((R, H), BF16),
        pltpu.VMEM((NCH, 4, RK, DQ), F32),
        pltpu.VMEM((NCH, 4, RK, DQ), BF16),
        pltpu.VMEM((NCH, 4, RK, DQ), BF16),
        pltpu.VMEM((NCH, RK, DQ), F32),
        pltpu.VMEM((NCH, 2, RG, DQ), BF16),
        pltpu.VMEM((NCH, 2, RG, DQ), BF16),
        pltpu.VMEM((NCH, 2, RK, DQ), BF16),
        pltpu.VMEM((NCH, 2, RK, DQ), BF16),
        pltpu.VMEM((NCH, RK, DQ), BF16),
        pltpu.VMEM((K * CAP, DQ), BF16),
        pltpu.VMEM((1, D), F32),
        pltpu.VMEM((1, D), F32),
        pltpu.VMEM((8, 1, 2 * D + 3 * 128), F32),
        pltpu.VMEM((K, 1, 128), F32),
        pltpu.VMEM((1, H), F32),
        pltpu.VMEM((1, D), F32),
        pltpu.VMEM((1, H), F32),
        dma((10,)), dma((1,)),
        dma((1,)), dma((1,)),
        dma((Z, Y)), dma((Z, Y)),
        dma((Y,)), dma((Y,)),
        dma((1,)), dma((1,)),
        dma((Z, 2)), dma((Z, 2)),
        dma((Z, 2)), dma((Z, 2)),
        dma((Z, 4)), dma((Z, 4)),
        dma((NCH,)), dma((NCH,)),
        dma((NCH, 2)), dma((NCH, 2)),
        dma((NCH, 2)), dma((NCH, 2)),
        dma((Z, Y)), dma((Z, Y)),
        dma((4, 2)), dma((4, 2)),
        dma((K,)), dma((K,)),
        dma((4 + H // 128,)),
    ]
    results = pl.pallas_call(
        functools.partial(kernel, (T, D, H, Z, Y)),
        out_shape=tuple(
            pltpu.VMEM(shape, dtype)
            for shape, dtype in (
                ((T, DQ), BF16),
                (w_in.shape, BF16),
                (w_out.shape, BF16),
                (in_row_mom.shape, F32),
                (in_col_mom.shape, F32),
                (out_row_mom.shape, F32),
                (out_col_mom.shape, F32),
            )
        ),
        in_specs=[hbm, hbm, vmem, hbm, hbm, vmem, vmem, vmem, vmem],
        out_specs=(vmem, hbm, hbm, vmem, vmem, vmem, vmem),
        scratch_shapes=scratch,
        compiler_params=pltpu.CompilerParams(
            collective_id=0, has_side_effects=True, vmem_limit_bytes=52 * 1024 * 1024
        ),
    )(
        tokens, out_grad, expert_ids.reshape(1, T), w_in, w_out,
        in_row_mom, in_col_mom, out_row_mom, out_col_mom,
    )
    return pl.pallas_call(
        deliver,
        out_shape=tuple(jax.ShapeDtypeStruct(r.shape, r.dtype) for r in results),
        in_specs=[hbm] * 7,
        out_specs=(hbm,) * 7,
        scratch_shapes=[dma((13,))],
        compiler_params=pltpu.CompilerParams(vmem_limit_bytes=1024 * 1024),
    )(*results)


def solution(mesh):
    placed = (
        P("expert", None),
        P("expert", None),
        P("expert", None),
        P("expert", None, "mp"),
        P("expert", "mp", None),
        P("expert", None),
        P("expert", "mp"),
        P("expert", "mp"),
        P("expert", None),
    )
    return jax.shard_map(
        shards,
        mesh=mesh,
        in_specs=placed,
        out_specs=(
            P("expert", "mp"),
            P("expert", None, "mp"),
            P("expert", "mp", None),
            P("expert", None),
            P("expert", "mp"),
            P("expert", "mp"),
            P("expert", None),
        ),
        check_vma=False,
    )
```
